512 devices in a mesh: row: 32 (over z, core), col: 16 (over y, x).
Axes of the slice: x: 4, y: 4, z: 16, core: 2. Of those that a mesh axis runs over, the one named last changes fastest.
Arguments:
- coeffs: bfloat16 [4096, 64, 128], P(('row', 'col')), may hold values from -6 to 6
- blocks: bfloat16 [262144, 64, 64], P(('row', 'col')), may hold values from -0.046875 to 0.046875
- blk_rows: int32 [262144], P(('row', 'col')), may hold values from 0 to 4095, as said below
- blk_cols: int32 [262144], P(('row', 'col')), may hold values from 0 to 4095, as said below
- blk_count: int32 [512], P(('row', 'col')), may hold values from 0 to 512, as said below
Outputs:
- product: float32 [4096, 64, 128], P(('row', 'col'))
The draws below stay inside these ranges and needn't reach their ends.
Inputs may be any that keep to these rules, and one draw needn't show every extreme that they name: `blk_rows`: element e belongs to device e // 8 in row+col order. In the first blk_count slots of a device, I <= J, I belongs to a device of the same row index, and J to a device of the same column index whose row index exceeds that of I's device by 0 to 3; the difference 3 occurs in every draw. Later slots hold elements of the device's own row and column groups and are unused; pairs may repeat. `blk_cols`: see blk_rows. `blk_count`: counts differ widely between devices; some device uses all 512 slots in every draw.
All inputs are finite; a program needn't handle non-finite values.
Results may differ from the reference program's by a relative error of at most 0.0003.
Values may be sent and summed in bfloat16 or wider, within the bound.
A program may use at most 128 MiB of HBM per device.

```python
import jax
import jax.numpy as jnp
from jax import lax

K = 64
NRHS = 128
ELEM_DEV = 8
BLK_DEV = 512
REACH = 3
ELEMS = 4096
N_ROW = 32
N_COL = 16
DEVICES = 512


def layout(key):
    base = jax.random.fold_in(key, 4321)
    keys = jax.random.split(base, 6)
    device = jnp.arange(DEVICES, dtype=jnp.int32)[:, None]
    row_index = device // N_COL
    col_index = device % N_COL
    segment = ELEM_DEV * N_COL
    shape = (DEVICES, BLK_DEV)
    slots = jnp.arange(BLK_DEV, dtype=jnp.int32)[None, :]
    last_slot = (device == DEVICES - 1) & (slots == 0)
    row_elems = row_index * segment + jax.random.randint(keys[0], shape, 0, segment)
    row_elems = jnp.where(last_slot, ELEMS - 1, row_elems)
    offset = jax.random.randint(keys[1], shape, 0, REACH + 1)
    inside_block = jax.random.randint(keys[2], shape, 0, ELEM_DEV)
    inside_block = jnp.where(last_slot, ELEM_DEV - 1, inside_block)
    full_col = jax.random.randint(keys[3], (), 0, N_COL)
    offset = jnp.where((device == full_col) & (slots == 0), REACH, offset)
    first = (row_index * N_COL + col_index) * ELEM_DEV + inside_block
    offset = jnp.where((offset == 0) & (first < row_elems), REACH, offset)
    usable = row_index + offset <= N_ROW - 1
    col_elems = ((row_index + offset) * N_COL + col_index) * ELEM_DEV + inside_block
    col_elems = jnp.where(usable, col_elems, first)
    order = jnp.argsort(1 - usable.astype(jnp.int32), axis=1, stable=True)
    row_elems = jnp.take_along_axis(row_elems, order, axis=1)
    col_elems = jnp.take_along_axis(col_elems, order, axis=1)
    usable_total = jnp.sum(usable.astype(jnp.int32), axis=1)
    lowest = max(BLK_DEV // 16, 1)
    first_draw = jax.random.randint(keys[4], (DEVICES,), lowest, BLK_DEV + 1)
    second_draw = jax.random.randint(keys[5], (DEVICES,), lowest, BLK_DEV + 1)
    totals = jnp.minimum(first_draw, second_draw)
    totals = jnp.where(jnp.arange(DEVICES, dtype=jnp.int32) == full_col, BLK_DEV, totals)
    totals = jnp.minimum(totals, usable_total)
    return (row_elems.reshape(-1).astype(jnp.int32), col_elems.reshape(-1).astype(jnp.int32), totals.astype(jnp.int32))


def draw_blk_rows(key, part):
    return layout(key)[0]


def draw_blk_cols(key, part):
    return layout(key)[1]


def draw_blk_count(key, part):
    return layout(key)[2]


def block_scale(stream_key, dims, cuts, low, high):
    level = 1.0
    for position, parts in cuts:
        draws = jax.random.uniform(jax.random.fold_in(jax.random.fold_in(stream_key, 6), position), (parts,), jnp.float32, low / len(cuts), high / len(cuts))
        level = level * jnp.repeat(jnp.exp(draws), dims[position] // parts).reshape((-1,) + (1,) * (len(dims) - 1 - position))
    return level


def scatter_about(stream_key, extent, spread, limit, shards=(), kind=jnp.bfloat16):
    entries = spread * jax.random.normal(stream_key, extent, jnp.float32)
    if shards:
        entries = entries * block_scale(stream_key, extent, shards, -0.22, 0.18)
    return jnp.clip(entries, -limit, limit).astype(kind)


def setup_inputs(seed: int = 0) -> dict:
    splits = jax.random.split(jax.random.key(seed), 6)
    coeffs = scatter_about(splits[0], (ELEMS, K, NRHS), 1.0, 6.0, ((0, 512),))
    blocks = scatter_about(splits[1], (DEVICES * BLK_DEV, K, K), (K * BLK_DEV // 2) ** -0.5, 0.046875, ((0, 512),))
    blk_rows = draw_blk_rows(jax.random.fold_in(splits[5], 71), 0)
    blk_cols = draw_blk_cols(jax.random.fold_in(splits[5], 71), 0)
    blk_count = draw_blk_count(jax.random.fold_in(splits[5], 71), 0)
    return {"coeffs": coeffs, "blocks": blocks, "blk_rows": blk_rows, "blk_cols": blk_cols, "blk_count": blk_count}


def reference(coeffs, blocks, blk_rows, blk_cols, blk_count):
    high_precision = lax.Precision.HIGHEST
    segment = ELEM_DEV * N_COL
    all_blocks = blocks.reshape(DEVICES, BLK_DEV, K, K)
    all_rows = blk_rows.reshape(DEVICES, BLK_DEV)
    all_cols = blk_cols.reshape(DEVICES, BLK_DEV)
    slots = jnp.arange(BLK_DEV, dtype=jnp.int32)
    devices = jnp.arange(DEVICES, dtype=jnp.int32)
    seg_index = jnp.arange(segment, dtype=jnp.int32)

    def visit(total, inputs):
        upper_block_list, row_ids, column_numbers, used, device = inputs
        active = slots < used
        mirror = active & (row_ids != column_numbers)
        upper_block_list = upper_block_list.astype(jnp.float32)
        column_entries = coeffs[column_numbers].astype(jnp.float32)
        row_entries = coeffs[row_ids].astype(jnp.float32)
        row_contributions = jnp.einsum("gjc,gcx->gjx", upper_block_list, column_entries, precision=high_precision)
        column_contributions = jnp.einsum("ihv,ihe->ive", upper_block_list, row_entries, precision=high_precision)
        row_contributions = row_contributions * active.astype(jnp.float32)[:, None, None]
        column_contributions = column_contributions * mirror.astype(jnp.float32)[:, None, None]
        base = ((device // N_COL) * segment).astype(jnp.int32)
        row_local = jnp.clip(row_ids - base, 0, segment - 1).astype(jnp.int32)
        partial_value = jnp.zeros((segment, K, NRHS), jnp.float32).at[row_local].add(row_contributions)
        total = total.at[base + seg_index].add(partial_value)
        total = total.at[column_numbers].add(column_contributions)
        return total, None

    start = jnp.zeros((ELEMS, K, NRHS), jnp.float32)
    total, _ = lax.scan(visit, start, (all_blocks, all_rows, all_cols, blk_count, devices))
    return total
```

```python
import jax
import jax.numpy as jnp
from jax import lax
from jax.experimental import pallas as pl
from jax.experimental.pallas import tpu as pltpu
from jax.sharding import PartitionSpec as P

MESH = pl.DeviceIdType.MESH
F32, BF16, I16, I32 = jnp.float32, jnp.bfloat16, jnp.int16, jnp.int32

K = 64
NRHS = 128
ELEM = 8
SLOTS = 512
HALF = SLOTS // 2
REACH = 3
SIDE = 4
COLS = SIDE * SIDE
GROUP = ELEM * COLS
WINDOW = ELEM * (REACH + 1)
QUART = ELEM // 2
UNROLL = 16
STEP = 32767.0

T_COL, T_ROW = 0, SLOTS
T_PREV_ROW, T_PREV_COL = 2 * SLOTS, 3 * SLOTS
T_LAST_ROW = 4 * SLOTS
T_LAST_COL = T_LAST_ROW + 2 * GROUP


def nn(a, b):
    return lax.dot_general(a, b, (((1,), (0,)), ((), ())), preferred_element_type=F32)


def nt(a, b):
    return lax.dot_general(a, b, (((1,), (1,)), ((), ())), preferred_element_type=F32)


def add_terms(terms, table, prev, hist):
    for p, one, two in terms:
        hist[p] = one + hist[table[prev + p]]
        hist[p + HALF] = two + hist[table[prev + HALF + p]]


def row_terms(i, table, near, mats, hist):
    zero = jnp.zeros((K, NRHS), BF16)
    terms = []
    for u in range(UNROLL):
        p = i * UNROLL + u
        one, two = near[table[T_COL + p]], near[table[T_COL + HALF + p]]
        pair = mats[pl.ds(pl.multiple_of(p * K, K), K), :].astype(BF16)
        both = jnp.concatenate(
            [jnp.concatenate([one, zero], 1), jnp.concatenate([zero, two], 1)], 0
        )
        t = nn(pair, both)
        terms.append((p, t[:, :NRHS], t[:, NRHS:]))
    add_terms(terms, table, T_PREV_ROW, hist)


def col_terms(i, table, group, mats, hist):
    terms = []
    for u in range(UNROLL):
        p = i * UNROLL + u
        one, two = group[table[T_ROW + p]], group[table[T_ROW + HALF + p]]
        pair = mats[pl.ds(pl.multiple_of(p * K, K), K), :].T.astype(BF16)
        terms.append((p, nn(pair[:K], one), nn(pair[K:], two)))
    add_terms(terms, table, T_PREV_COL, hist)


def total(table, first, size, e, hist):
    return hist[table[first + e]] + hist[table[first + size + e]]


def coded(value):
    peak = jnp.max(jnp.abs(value), axis=0, keepdims=True)
    safe = jnp.maximum(peak, 1e-30)
    codes = jnp.round(value * (STEP / safe)).astype(I32).astype(I16)
    return codes, safe * (1.0 / STEP)


def decoded(codes, step):
    return codes.astype(I32).astype(F32) * step


def kernel(
    table, coeffs, blocks, out,
    flat, mats, hist, group, near, own, mine,
    send1, step1, got1, gstep1, send2, step2, got2, gstep2,
    sendc, stepc, gotc, gstepc,
    load_sem, ag_send, ag_recv, win_send, win_recv, s1_send, s1_recv, s2_send, s2_recv, c_send, c_recv,
):
    row, col = lax.axis_index("row"), lax.axis_index("col")
    n_row = lax.axis_size("row")
    at = (lax.rem(col, SIDE), lax.div(col, SIDE))

    def place(k, a, b):
        return b * SIDE + a if k == 0 else a * SIDE + b

    def shift(v, by):
        return lax.rem(v + by + SIDE, SIDE)

    def send(src, dst, s, r, device):
        return pltpu.make_async_remote_copy(
            src_ref=src, dst_ref=dst, send_sem=s, recv_sem=r, device_id=device, device_id_type=MESH
        )

    chunk = K * K // 4
    loads = [
        pltpu.make_async_copy(
            blocks.at[pl.ds(i * chunk, chunk)], flat.at[pl.ds(i * chunk, chunk)], load_sem.at[i]
        )
        for i in range(4)
    ]
    for c in loads:
        c.start()
    group[pl.ds(pl.multiple_of(col * ELEM, ELEM), ELEM)] = coeffs[...]
    near[pl.ds(0, ELEM)] = coeffs[...]
    near[pl.ds(ELEM, WINDOW - ELEM)] = jnp.zeros((WINDOW - ELEM, K, NRHS), BF16)
    gotc[...] = jnp.zeros_like(gotc)
    gstepc[...] = jnp.zeros_like(gstepc)

    barrier = pltpu.get_barrier_semaphore()
    for k in range(2):
        for by in range(1, SIDE):
            peer = place(k, shift(at[k], by), at[1 - k])
            pl.semaphore_signal(barrier, inc=1, device_id={"col": peer}, device_id_type=MESH)
    count = 2 * (SIDE - 1)
    for o in range(1, REACH + 1):
        for r in (row - o, row + o):
            inside = (r >= 0) & (r < n_row)

            @pl.when(inside)
            def _(r=r):
                pl.semaphore_signal(barrier, inc=1, device_id={"row": r}, device_id_type=MESH)

            count = count + jnp.where(inside, 1, 0)
    pl.semaphore_wait(barrier, count)

    def window(o, peer):
        return send(
            coeffs, near.at[pl.ds(o * ELEM, ELEM)], win_send.at[o - 1], win_recv.at[o - 1], {"row": peer}
        )

    for o in range(1, REACH + 1):

        @pl.when(row - o >= 0)
        def _(o=o):
            window(o, row - o).start()

    def piece(k, da, db, part=None):
        dev = place(k, shift(at[k], da), shift(at[1 - k], db))
        if part is None:
            return group.at[pl.ds(dev * ELEM + k * QUART, QUART)]
        return group.at[pl.ds(dev * ELEM + k * QUART + part * (QUART // 2), QUART // 2)]

    started = []

    def gather(k, axis, da, db, part, to, index):
        a, b = (shift(at[k], to), at[1 - k]) if axis == 0 else (at[k], shift(at[1 - k], to))
        ref = piece(k, da, db, part)
        c = send(ref, ref, ag_send.at[k, index], ag_recv.at[k, index], {"col": place(k, a, b)})
        c.start()
        started.append(c)

    def arrived(k, da, db, part, index):
        ref = piece(k, da, db, part)
        send(ref, ref, ag_send.at[k, index], ag_recv.at[k, index], {"col": col}).wait_recv()

    def along(k, da):
        q = (0, 2, 3, 1)[da + 0] if da >= 0 else 1
        gather(k, 1, da, 0, None, 1, 4 + 4 * q)
        gather(k, 1, da, 0, None, -1, 5 + 4 * q)

    def across(k, da):
        q = (0, 2, 3, 1)[da + 0] if da >= 0 else 1
        arrived(k, da, -1, None, 4 + 4 * q)
        gather(k, 1, da, -1, 0, 1, 6 + 4 * q)
        arrived(k, da, 1, None, 5 + 4 * q)
        gather(k, 1, da, 1, 1, -1, 7 + 4 * q)

    def last(k, da):
        q = (0, 2, 3, 1)[da + 0] if da >= 0 else 1
        arrived(k, da, 2, 0, 6 + 4 * q)
        arrived(k, da, 2, 1, 7 + 4 * q)

    for k in range(2):
        gather(k, 0, 0, 0, None, 1, 0)
        gather(k, 0, 0, 0, None, -1, 1)
    for k in range(2):
        along(k, 0)

    r = lax.broadcasted_iota(I32, (HALF, HALF), 0)
    c = lax.broadcasted_iota(I32, (HALF, HALF), 1)
    eye = jnp.where(r == c, 1.0, 0.0).astype(BF16)

    def turn(i, _):
        for u in range(8):
            j = i * 8 + u
            a = flat[pl.ds(pl.multiple_of(j * K, K), K), :]
            a = jnp.concatenate([a[:, :HALF], a[:, HALF:]], axis=0)
            mats[pl.ds(j, HALF, stride=K), :] = nt(eye, a)
        return 0

    loads[0].wait()
    loads[1].wait()
    lax.fori_loop(0, 4, turn, 0)
    for k in range(2):
        arrived(k, -1, 0, None, 0)
        gather(k, 0, -1, 0, 0, 1, 2)
        arrived(k, 1, 0, None, 1)
        gather(k, 0, 1, 0, 1, -1, 3)
        along(k, -1)
        along(k, 1)
    loads[2].wait()
    loads[3].wait()
    lax.fori_loop(4, 8, turn, 0)
    for k in range(2):
        arrived(k, 2, 0, 0, 2)
        arrived(k, 2, 0, 1, 3)
        along(k, 2)
        across(k, 0)

    for o in range(1, REACH + 1):

        @pl.when(row + o < n_row)
        def _(o=o):
            window(o, row).wait_recv()

    hist[SLOTS] = jnp.zeros((K, NRHS), F32)

    def rows(i, _):
        row_terms(i, table, near, mats, hist)
        return 0

    steps = HALF // UNROLL
    lax.fori_loop(0, steps // 2, rows, 0)
    for k in range(2):
        across(k, -1)
        across(k, 1)
    lax.fori_loop(steps // 2, steps, rows, 0)
    for k in range(2):
        across(k, 2)

    def first(k, d, peer):
        return (
            send(send1.at[k, d], got1.at[k, d], s1_send.at[k, d, 0], s1_recv.at[k, d, 0], {"col": peer}),
            send(step1.at[k, d], gstep1.at[k, d], s1_send.at[k, d, 1], s1_recv.at[k, d, 1], {"col": peer}),
        )

    for d in (1, 0, 2):
        for k in range(2):
            a = shift(at[k], d + 1)

            def code(i, _, k=k, d=d, a=a):
                base = place(k, a, i) * ELEM + k * QUART
                for u in range(QUART):
                    codes, step = coded(total(table, T_LAST_ROW, GROUP, base + u, hist))
                    send1[k, d, i, u] = codes
                    step1[k, d, i, pl.ds(u, 1)] = step
                return 0

            lax.fori_loop(0, SIDE, code, 0)
            for c in first(k, d, place(k, a, at[1 - k])):
                c.start()
    for k in range(2):

        def keep(i, _, k=k):
            base = place(k, at[k], i) * ELEM + k * QUART
            for u in range(QUART):
                own[k, i, u] = total(table, T_LAST_ROW, GROUP, base + u, hist)
            return 0

        lax.fori_loop(0, SIDE, keep, 0)

    for k in range(2):
        for da in (0, -1, 1, 2):
            last(k, da)

    def cols(i, _):
        col_terms(i, table, group, mats, hist)
        return 0

    lax.fori_loop(0, steps, cols, 0)

    def column(o, peer):
        return (
            send(sendc.at[o - 1], gotc.at[o - 1], c_send.at[o - 1, 0], c_recv.at[o - 1, 0], {"row": peer}),
            send(stepc.at[o - 1], gstepc.at[o - 1], c_send.at[o - 1, 1], c_recv.at[o - 1, 1], {"row": peer}),
        )

    for o in range(1, REACH + 1):
        for u in range(ELEM):
            codes, step = coded(total(table, T_LAST_COL, WINDOW, o * ELEM + u, hist))
            sendc[o - 1, u] = codes
            stepc[o - 1, pl.ds(u, 1)] = step

        @pl.when(row + o < n_row)
        def _(o=o):
            for c in column(o, row + o):
                c.start()

    for u in range(ELEM):
        mine[u] = total(table, T_LAST_COL, WINDOW, u, hist)

    def second(k, d, peer):
        return (
            send(send2.at[k, d], got2.at[k, d], s2_send.at[k, d, 0], s2_recv.at[k, d, 0], {"col": peer}),
            send(step2.at[k, d], gstep2.at[k, d], s2_send.at[k, d, 1], s2_recv.at[k, d, 1], {"col": peer}),
        )

    def gathered(k, b, u):
        v = own[k, b, u]
        for d in range(SIDE - 1):
            v = v + decoded(got1[k, d, b, u], gstep1[k, d, b, pl.ds(u, 1)])
        return v

    for k in range(2):
        for d in range(SIDE - 1):
            for c in first(k, d, col):
                c.wait_recv()
        for d in (1, 0, 2):
            b = shift(at[1 - k], d + 1)
            for u in range(QUART):
                codes, step = coded(gathered(k, b, u))
                send2[k, d, u] = codes
                step2[k, d, pl.ds(u, 1)] = step
            for c in second(k, d, place(k, at[k], b)):
                c.start()
    for k in range(2):
        for u in range(QUART):
            mine[k * QUART + u] += gathered(k, at[1 - k], u)

    for o in range(1, REACH + 1):

        @pl.when(row - o >= 0)
        def _(o=o):
            for c in column(o, row):
                c.wait_recv()

    for u in range(ELEM):
        v = mine[u]
        for o in range(REACH):
            v = v + decoded(gotc[o, u], gstepc[o, pl.ds(u, 1)])
        mine[u] = v
    for k in range(2):
        for d in range(SIDE - 1):
            for c in second(k, d, col):
                c.wait_recv()
        for u in range(QUART):
            v = mine[k * QUART + u]
            for d in range(SIDE - 1):
                v = v + decoded(got2[k, d, u], gstep2[k, d, pl.ds(u, 1)])
            out[k * QUART + u] = v

    for c in started:
        c.wait_send()
    for k in range(2):
        for d in range(SIDE - 1):
            for c in (*first(k, d, col), *second(k, d, col)):
                c.wait_send()
    for o in range(1, REACH + 1):

        @pl.when(row - o >= 0)
        def _(o=o):
            window(o, row).wait_send()

        @pl.when(row + o < n_row)
        def _(o=o):
            for c in column(o, row):
                c.wait_send()


def chains(keys, size):
    slots = jnp.arange(SLOTS, dtype=I32)
    before = (slots[None, :] < slots[:, None]) & (slots[None, :] // HALF == slots[:, None] // HALF)
    same = (keys[None, :] == keys[:, None]) & before
    prev = jnp.max(jnp.where(same, slots[None, :], -1), axis=1)
    names = jnp.arange(size, dtype=I32)
    halves = jnp.arange(2, dtype=I32)
    here = (keys[None, None, :] == names[None, :, None]) & (slots[None, None, :] // HALF == halves[:, None, None])
    last = jnp.max(jnp.where(here, slots[None, None, :], -1), axis=2).reshape(-1)
    return jnp.where(prev < 0, SLOTS, prev), jnp.where(last < 0, SLOTS, last)


def body(coeffs, blocks, blk_rows, blk_cols, blk_count):
    my_row = lax.axis_index("row")
    slots = jnp.arange(SLOTS, dtype=I32)
    active = slots < blk_count[0]
    mirror = active & (blk_rows != blk_cols)
    row_local = jnp.clip(blk_rows - my_row * GROUP, 0, GROUP - 1)
    col_local = (blk_cols // GROUP - my_row) * ELEM + blk_cols % ELEM
    col_local = jnp.clip(col_local, 0, WINDOW - 1)
    prev_row, last_row = chains(jnp.where(active, row_local, -1), GROUP)
    prev_col, last_col = chains(jnp.where(mirror, col_local, -1), WINDOW)
    table = jnp.concatenate([col_local, row_local, prev_row, prev_col, last_row, last_col])
    flat = jnp.transpose(blocks, (1, 2, 0)).reshape(K * K, SLOTS)
    side = SIDE - 1
    vmem, dma = pltpu.VMEM, pltpu.SemaphoreType.DMA
    return pl.pallas_call(
        kernel,
        out_shape=jax.ShapeDtypeStruct((ELEM, K, NRHS), F32),
        in_specs=[
            pl.BlockSpec(memory_space=pltpu.SMEM),
            pl.BlockSpec(memory_space=pltpu.VMEM),
            pl.BlockSpec(memory_space=pl.ANY),
        ],
        out_specs=pl.BlockSpec(memory_space=pltpu.VMEM),
        scratch_shapes=[
            vmem((K * K, SLOTS), BF16),
            vmem((HALF * K, 2 * K), F32),
            vmem((SLOTS + 1, K, NRHS), F32),
            vmem((GROUP, K, NRHS), BF16),
            vmem((WINDOW, K, NRHS), BF16),
            vmem((2, SIDE, QUART, K, NRHS), F32),
            vmem((ELEM, K, NRHS), F32),
            vmem((2, side, SIDE, QUART, K, NRHS), I16),
            vmem((2, side, SIDE, ELEM, NRHS), F32),
            vmem((2, side, SIDE, QUART, K, NRHS), I16),
            vmem((2, side, SIDE, ELEM, NRHS), F32),
            vmem((2, side, QUART, K, NRHS), I16),
            vmem((2, side, ELEM, NRHS), F32),
            vmem((2, side, QUART, K, NRHS), I16),
            vmem((2, side, ELEM, NRHS), F32),
            vmem((REACH, ELEM, K, NRHS), I16),
            vmem((REACH, ELEM, NRHS), F32),
            vmem((REACH, ELEM, K, NRHS), I16),
            vmem((REACH, ELEM, NRHS), F32),
            dma((4,)),
            dma((2, 20)),
            dma((2, 20)),
            dma((REACH,)),
            dma((REACH,)),
            dma((2, side, 2)),
            dma((2, side, 2)),
            dma((2, side, 2)),
            dma((2, side, 2)),
            dma((REACH, 2)),
            dma((REACH, 2)),
        ],
        compiler_params=pltpu.CompilerParams(
            collective_id=0, has_side_effects=True, vmem_limit_bytes=56 * 2**20
        ),
        name="near_field",
    )(table, coeffs, flat)


def solution(mesh):
    placed = (
        P(("row", "col"), None, None),
        P(("row", "col"), None, None),
        P(("row", "col")),
        P(("row", "col")),
        P(("row", "col")),
    )
    return jax.shard_map(
        body, mesh=mesh, in_specs=placed, out_specs=P(("row", "col"), None, None), check_vma=False
    )
```

```python
import jax
import jax.numpy as jnp
from jax import lax
from jax.experimental import pallas as pl
from jax.experimental.pallas import tpu as pltpu
from jax.sharding import PartitionSpec as P

MESH = pl.DeviceIdType.MESH
F32, BF16, I16, I32 = jnp.float32, jnp.bfloat16, jnp.int16, jnp.int32

K = 64
NRHS = 128
ELEM = 8
SLOTS = 512
HALF = SLOTS // 2
REACH = 3
SIDE = 4
COLS = SIDE * SIDE
GROUP = ELEM * COLS
WINDOW = ELEM * (REACH + 1)
QUART = ELEM // 2
UNROLL = 16
STEP = 32767.0
EXTRA = 16

LANES = 128
TILES = SLOTS // LANES
T_COL, T_ROW, T_PREV_ROW, T_PREV_COL = 0, TILES, 2 * TILES, 3 * TILES
T_LAST_ROW, T_LAST_COL = 4 * TILES, 4 * TILES + 2
T_ROWS = 4 * TILES + 8


def nn(a, b):
    return lax.dot_general(a, b, (((1,), (0,)), ((), ())), preferred_element_type=F32)


def nt(a, b):
    return lax.dot_general(a, b, (((1,), (1,)), ((), ())), preferred_element_type=F32)


def entry(table, name, i, u, half):
    per = LANES // UNROLL
    return table[name + half * (TILES // 2) + lax.div(i, per), lax.rem(i, per) * UNROLL + u]


def add_terms(i, terms, table, prev, hist):
    for u, pair in enumerate(terms):
        for half, term in enumerate(pair):
            hist[half * HALF + i * UNROLL + u] = term + hist[entry(table, prev, i, u, half)]


def row_terms(i, table, near, mats, hist):
    zero = jnp.zeros((K, NRHS), BF16)
    terms = []
    for u in range(UNROLL):
        one, two = (near[entry(table, T_COL, i, u, half)] for half in range(2))
        pair = mats[pl.ds(pl.multiple_of((i * UNROLL + u) * K, K), K), :].astype(BF16)
        both = jnp.concatenate(
            [jnp.concatenate([one, zero], 1), jnp.concatenate([zero, two], 1)], 0
        )
        t = nn(pair, both)
        terms.append((t[:, :NRHS], t[:, NRHS:]))
    add_terms(i, terms, table, T_PREV_ROW, hist)


def col_terms(i, table, group, mats, hist):
    terms = []
    for u in range(UNROLL):
        one, two = (group[entry(table, T_ROW, i, u, half)] for half in range(2))
        pair = mats[pl.ds(pl.multiple_of((i * UNROLL + u) * K, K), K), :].T.astype(BF16)
        terms.append((nn(pair[:K], one), nn(pair[K:], two)))
    add_terms(i, terms, table, T_PREV_COL, hist)


def total(table, name, e, hist):
    return hist[table[name, e]] + hist[table[name + 1, e]]


def tables(count_ref, rows_ref, cols_ref, out):
    rows, cols, count = rows_ref[...], cols_ref[...], count_ref[0]
    my_row = lax.axis_index("row")
    slot = lax.broadcasted_iota(I32, (TILES, LANES), 0) * LANES + lax.broadcasted_iota(I32, (TILES, LANES), 1)
    active = slot < count
    mirror = active & (rows != cols)
    row_local = jnp.clip(rows - my_row * GROUP, 0, GROUP - 1)
    col_local = (lax.shift_right_logical(cols, 7) - my_row) * ELEM + (cols & (ELEM - 1))
    col_local = jnp.clip(col_local, 0, WINDOW - 1)
    out[pl.ds(T_COL, TILES)] = col_local
    out[pl.ds(T_ROW, TILES)] = row_local
    out[pl.ds(T_LAST_COL + 2, T_ROWS - T_LAST_COL - 2)] = jnp.zeros((T_ROWS - T_LAST_COL - 2, LANES), I32)
    down = lax.broadcasted_iota(I32, (LANES, LANES), 0)
    across = lax.broadcasted_iota(I32, (LANES, LANES), 1)
    names = across.astype(F32)
    for key, prev, last in (
        (jnp.where(active, row_local, -1), T_PREV_ROW, T_LAST_ROW),
        (jnp.where(mirror, col_local, -1), T_PREV_COL, T_LAST_COL),
    ):
        key = key.astype(F32)
        wide = [jnp.broadcast_to(key[t : t + 1], (LANES, LANES)) for t in range(TILES)]
        tall = [w.T for w in wide]
        number = [(down + t * LANES).astype(F32) for t in range(TILES)]
        none = jnp.full((LANES, LANES), -1.0, F32)
        for half in range(2):
            low, high = 2 * half, 2 * half + 1
            found = []
            found.append(jnp.where((tall[low] == wide[low]) & (down < across), number[low], none))
            found.append(
                jnp.maximum(
                    jnp.where(tall[low] == wide[high], number[low], none),
                    jnp.where((tall[high] == wide[high]) & (down < across), number[high], none),
                )
            )
            ends = jnp.maximum(
                jnp.where(tall[low] == names, number[low], none),
                jnp.where(tall[high] == names, number[high], none),
            )
            for place, f in ((prev + low, found[0]), (prev + high, found[1]), (last + half, ends)):
                best = jnp.max(f, axis=0, keepdims=True)
                out[pl.ds(place, 1)] = jnp.where(best < 0, float(SLOTS), best).astype(I32)


def coded(values, out):
    n = len(values)
    peaks = [jnp.max(jnp.abs(v), axis=0, keepdims=True) for v in values]
    peaks.append(jnp.ones((EXTRA - n, NRHS), F32))
    power = jnp.ceil(jnp.log2(jnp.maximum(jnp.concatenate(peaks, axis=0), 1e-30)))
    out[pl.ds(n * K, EXTRA)] = power.astype(I32).astype(I16)
    scale = jnp.exp2(-power) * STEP
    for u, v in enumerate(values):
        out[pl.ds(u * K, K)] = jnp.round(v * scale[u : u + 1]).astype(I32).astype(I16)


def decoded(codes, n):
    step = jnp.exp2(codes[pl.ds(n * K, EXTRA)].astype(I32).astype(F32)) * (1.0 / STEP)
    return [codes[pl.ds(u * K, K)].astype(I32).astype(F32) * step[u : u + 1] for u in range(n)]


def kernel(
    table, coeffs, blocks, out, out_cols,
    flat, mats, hist, group, near, own,
    send1, got1, send2, got2, sendc, gotc, swap_out, swap_in, beside_out, beside_in,
    load_sem, ag_send, ag_recv, win_send, win_recv, s1_send, s1_recv, s2_send, s2_recv, c_send, c_recv,
):
    row, col = lax.axis_index("row"), lax.axis_index("col")
    n_row = lax.axis_size("row")
    core = lax.rem(row, 2)
    at = (lax.rem(col, SIDE), lax.div(col, SIDE))

    def place(k, a, b):
        return a * (1 + (SIDE - 1) * k) + b * (SIDE - (SIDE - 1) * k)

    def shift(v, by):
        return lax.rem(v + by + SIDE, SIDE)

    def send(src, dst, s, r, device):
        return pltpu.make_async_remote_copy(
            src_ref=src, dst_ref=dst, send_sem=s, recv_sem=r, device_id=device, device_id_type=MESH
        )

    barrier = pltpu.get_barrier_semaphore()
    for k in range(2):
        for by in range(1, SIDE):
            peer = place(k, shift(at[k], by), at[1 - k])
            pl.semaphore_signal(barrier, inc=1, device_id={"col": peer}, device_id_type=MESH)
    signals = 2 * (SIDE - 1)
    for o in range(1, REACH + 1):
        for r in (row - o, row + o):
            inside = (r >= 0) & (r < n_row)

            @pl.when(inside)
            def _(r=r):
                pl.semaphore_signal(barrier, inc=1, device_id={"row": r}, device_id_type=MESH)

            signals = signals + jnp.where(inside, 1, 0)

    chunk = K * K // 4
    loads = [
        pltpu.make_async_copy(
            blocks.at[pl.ds(i * chunk, chunk)], flat.at[pl.ds(i * chunk, chunk)], load_sem.at[i]
        )
        for i in range(4)
    ]
    for c in loads:
        c.start()
    group[pl.ds(pl.multiple_of(col * ELEM, ELEM), ELEM)] = coeffs[...]
    near[pl.ds(0, ELEM)] = coeffs[...]
    for o in range(1, REACH + 1):

        @pl.when(row + o >= n_row)
        def _(o=o):
            near[pl.ds(o * ELEM, ELEM)] = jnp.zeros((ELEM, K, NRHS), BF16)

    pl.semaphore_wait(barrier, signals)

    def window(o, src, s, peer):
        return send(src, near.at[pl.ds(o * ELEM, ELEM)], win_send.at[s], win_recv.at[o - 1], {"row": peer})

    second_row = near.at[pl.ds(2 * ELEM, ELEM)]
    passed = row + 2 < n_row
    windows = (
        (row >= 2, lambda: window(2, coeffs, 0, row - 2)),
        (core == 1, lambda: window(1, coeffs, 1, row - 1)),
        ((core == 0) & passed & (row >= 2), lambda: window(3, second_row, 1, row - 1)),
        ((core == 0) & passed, lambda: window(1, second_row, 2, row + 1)),
        ((core == 1) & passed, lambda: window(3, second_row, 2, row - 1)),
    )

    def window_arrived(o):
        @pl.when(row + o < n_row)
        def _():
            window(o, coeffs, 0, row).wait_recv()

    for when, make in windows[:2]:

        @pl.when(when)
        def _(make=make):
            make().start()

    def piece(k, da, db, part=None):
        dev = place(k, shift(at[k], da), shift(at[1 - k], db))
        if part is None:
            return group.at[pl.ds(dev * ELEM + k * QUART, QUART)]
        return group.at[pl.ds(dev * ELEM + k * QUART + part * (QUART // 2), QUART // 2)]

    started = []
    order = {0: 0, -1: 1, 1: 2, 2: 3}

    def gather(k, axis, da, db, part, to, index):
        a, b = (shift(at[k], to), at[1 - k]) if axis == 0 else (at[k], shift(at[1 - k], to))
        ref = piece(k, da, db, part)
        c = send(ref, ref, ag_send.at[k, index], ag_recv.at[k, index], {"col": place(k, a, b)})
        c.start()
        started.append(c)

    def arrived(k, da, db, part, index):
        ref = piece(k, da, db, part)
        send(ref, ref, ag_send.at[k, index], ag_recv.at[k, index], {"col": col}).wait_recv()

    def along(k, da):
        gather(k, 1, da, 0, None, 1, 3 + 4 * order[da])
        gather(k, 1, da, 0, None, -1, 4 + 4 * order[da])

    def across(k, da):
        arrived(k, da, -1, None, 3 + 4 * order[da])
        gather(k, 1, da, -1, 0, 1, 5 + 4 * order[da])
        arrived(k, da, 1, None, 4 + 4 * order[da])
        gather(k, 1, da, 1, 1, -1, 6 + 4 * order[da])

    def last(k, da):
        arrived(k, da, 2, 0, 5 + 4 * order[da])
        arrived(k, da, 2, 1, 6 + 4 * order[da])

    for k in range(2):
        gather(k, 0, 0, 0, None, 1, 0)
        gather(k, 0, 0, 0, None, -1, 1)
    for k in range(2):
        gather(k, 0, 0, 0, None, 2, 2)
    for k in range(2):
        along(k, 0)

    r = lax.broadcasted_iota(I32, (HALF, HALF), 0)
    c = lax.broadcasted_iota(I32, (HALF, HALF), 1)
    eye = jnp.where(r == c, 1.0, 0.0).astype(BF16)

    def turn(i, _):
        for u in range(8):
            j = i * 8 + u
            a = flat[pl.ds(pl.multiple_of(j * K, K), K), :]
            a = jnp.concatenate([a[:, :HALF], a[:, HALF:]], axis=0)
            mats[pl.ds(j, HALF, stride=K), :] = nt(eye, a)
        return 0

    for c in loads:
        c.wait()
    lax.fori_loop(0, 8, turn, 0)
    for k in range(2):
        arrived(k, -1, 0, None, 0)
        along(k, -1)
        arrived(k, 1, 0, None, 1)
        along(k, 1)
    window_arrived(2)
    for when, make in windows[2:]:

        @pl.when(when)
        def _(make=make):
            make().start()

    for k in range(2):
        arrived(k, 2, 0, None, 2)
        along(k, 2)
    for k in range(2):
        across(k, 0)
    window_arrived(1)
    window_arrived(3)

    hist[SLOTS] = jnp.zeros((K, NRHS), F32)

    def rows(i, _):
        row_terms(i, table, near, mats, hist)
        return 0

    steps = HALF // UNROLL
    lax.fori_loop(0, steps // 2, rows, 0)
    for k in range(2):
        across(k, -1)
        across(k, 1)
    lax.fori_loop(steps // 2, steps, rows, 0)
    for k in range(2):
        across(k, 2)

    def first(k, d, bo, peer):
        return send(
            send1.at[k, d, bo], got1.at[k, d, bo], s1_send.at[k, d, bo], s1_recv.at[k, d, bo], {"col": peer}
        )

    def pick(k):
        return at[0] * (1 - k) + at[1] * k, at[1] * (1 - k) + at[0] * k

    for bo in (2, 1, 3, 0):

        def code(i, _, bo=bo):
            k, d = lax.rem(i, 2), lax.rem(lax.div(i, 2) + 1, SIDE - 1)
            mine_a, mine_b = pick(k)
            a, b = shift(mine_a, d + 1), shift(mine_b, bo)
            base = place(k, a, b) * ELEM + k * QUART
            coded([total(table, T_LAST_ROW, base + u, hist) for u in range(QUART)], send1.at[k, d, bo])
            first(k, d, bo, place(k, a, mine_b)).start()
            return 0

        lax.fori_loop(0, 2 * (SIDE - 1), code, 0)

    def keep(i, _):
        k, bo = lax.div(i, SIDE), lax.rem(i, SIDE)
        mine_a, mine_b = pick(k)
        base = place(k, mine_a, shift(mine_b, bo)) * ELEM + k * QUART
        for u in range(QUART):
            own[k, bo, u] = total(table, T_LAST_ROW, base + u, hist)
        return 0

    lax.fori_loop(0, 2 * SIDE, keep, 0)

    for k in range(2):
        for da in (0, -1, 1, 2):
            last(k, da)

    def cols(i, _):
        col_terms(i, table, group, mats, hist)
        return 0

    lax.fori_loop(0, steps, cols, 0)

    def swap(peer):
        return send(swap_out, swap_in, c_send.at[0], c_recv.at[0], {"row": peer})

    def beside(peer):
        return send(beside_out, beside_in, c_send.at[1], c_recv.at[1], {"row": peer})

    def column(i, peer):
        return send(sendc.at[i], gotc.at[i], c_send.at[2 + i], c_recv.at[2 + i], {"row": peer})

    other = row + 1 - 2 * core
    for u in range(ELEM):
        swap_out[u] = total(table, T_LAST_COL, (3 - 2 * core) * ELEM + u, hist)

    @pl.when(passed)
    def _():
        swap(other).start()

    @pl.when((core == 1) & (row + 3 < n_row))
    def _():
        coded([total(table, T_LAST_COL, 3 * ELEM + u, hist) for u in range(ELEM)], sendc.at[1])
        column(1, row + 3).start()

    @pl.when(core == 0)
    def _():
        for u in range(ELEM):
            beside_out[u] = total(table, T_LAST_COL, ELEM + u, hist)
        beside(row + 1).start()

    for u in range(ELEM):
        out_cols[u] = total(table, T_LAST_COL, u, hist)

    @pl.when(passed)
    def _():
        swap(other).wait_recv()
        coded([total(table, T_LAST_COL, 2 * ELEM + u, hist) + swap_in[u] for u in range(ELEM)], sendc.at[0])
        column(0, row + 2).start()

    def second(k, d, peer):
        return send(send2.at[k, d], got2.at[k, d], s2_send.at[k, d], s2_recv.at[k, d], {"col": peer})

    def gathered(k, bo):
        for d in range(SIDE - 1):
            first(k, d, bo, col).wait_recv()
        parts = [decoded(got1.at[k, d, bo], QUART) for d in range(SIDE - 1)]
        return [own[k, bo, u] + parts[0][u] + parts[1][u] + parts[2][u] for u in range(QUART)]

    for bo in (2, 1, 3):
        for k in range(2):
            coded(gathered(k, bo), send2.at[k, bo - 1])
            second(k, bo - 1, place(k, at[k], shift(at[1 - k], bo))).start()
    for k in range(2):
        for u, v in enumerate(gathered(k, 0)):
            out[k * QUART + u] = v

    @pl.when(core == 1)
    def _():
        beside(row).wait_recv()
        for u in range(ELEM):
            out_cols[u] += beside_in[u]

    for i, when in ((1, (core == 0) & (row >= 3)), (0, row >= 2)):

        @pl.when(when)
        def _(i=i):
            column(i, row).wait_recv()
            for u, v in enumerate(decoded(gotc.at[i], ELEM)):
                out_cols[u] += v

    for k in range(2):
        for d in range(SIDE - 1):
            second(k, d, col).wait_recv()
        parts = [decoded(got2.at[k, d], QUART) for d in range(SIDE - 1)]
        for u in range(QUART):
            out[k * QUART + u] += parts[0][u] + parts[1][u] + parts[2][u]

    for c in started:
        c.wait_send()
    for k in range(2):
        for d in range(SIDE - 1):
            for bo in range(SIDE):
                first(k, d, bo, col).wait_send()
            second(k, d, col).wait_send()
    for when, make in windows:

        @pl.when(when)
        def _(make=make):
            make().wait_send()

    @pl.when(passed)
    def _():
        for c in (swap(other), column(0, row)):
            c.wait_send()

    @pl.when((core == 1) & (row + 3 < n_row))
    def _():
        column(1, row).wait_send()

    @pl.when(core == 0)
    def _():
        beside(row).wait_send()


def body(coeffs, blocks, blk_rows, blk_cols, blk_count):
    flat = jnp.transpose(blocks, (1, 2, 0)).reshape(K * K, SLOTS)
    side = SIDE - 1
    vmem, dma = pltpu.VMEM, pltpu.SemaphoreType.DMA
    table = pl.pallas_call(
        tables,
        out_shape=jax.ShapeDtypeStruct((T_ROWS, LANES), I32),
        in_specs=[
            pl.BlockSpec(memory_space=pltpu.SMEM),
            pl.BlockSpec(memory_space=pltpu.VMEM),
            pl.BlockSpec(memory_space=pltpu.VMEM),
        ],
        out_specs=pl.BlockSpec(memory_space=pltpu.VMEM),
        name="tables",
    )(blk_count, blk_rows.reshape(TILES, LANES), blk_cols.reshape(TILES, LANES))
    sums, columns = pl.pallas_call(
        kernel,
        out_shape=(jax.ShapeDtypeStruct((ELEM, K, NRHS), F32),) * 2,
        in_specs=[
            pl.BlockSpec(memory_space=pltpu.SMEM),
            pl.BlockSpec(memory_space=pltpu.VMEM),
            pl.BlockSpec(memory_space=pl.ANY),
        ],
        out_specs=(pl.BlockSpec(memory_space=pltpu.VMEM),) * 2,
        scratch_shapes=[
            vmem((K * K, SLOTS), BF16),
            vmem((HALF * K, 2 * K), F32),
            vmem((SLOTS + 1, K, NRHS), F32),
            vmem((GROUP, K, NRHS), BF16),
            vmem((WINDOW, K, NRHS), BF16),
            vmem((2, SIDE, QUART, K, NRHS), F32),
            *[vmem((2, side, SIDE, QUART * K + EXTRA, NRHS), I16)] * 2,
            *[vmem((2, side, QUART * K + EXTRA, NRHS), I16)] * 2,
            *[vmem((2, ELEM * K + EXTRA, NRHS), I16)] * 2,
            *[vmem((ELEM, K, NRHS), F32)] * 4,
            dma((4,)),
            dma((2, 19)),
            dma((2, 19)),
            dma((REACH,)),
            dma((REACH,)),
            dma((2, side, SIDE)),
            dma((2, side, SIDE)),
            dma((2, side)),
            dma((2, side)),
            dma((4,)),
            dma((4,)),
        ],
        compiler_params=pltpu.CompilerParams(
            collective_id=0, has_side_effects=True, vmem_limit_bytes=52 * 2**20
        ),
        name="near_field",
    )(table, coeffs, flat)
    return sums + columns


def solution(mesh):
    placed = (
        P(("row", "col"), None, None),
        P(("row", "col"), None, None),
        P(("row", "col")),
        P(("row", "col")),
        P(("row", "col")),
    )
    return jax.shard_map(
        body, mesh=mesh, in_specs=placed, out_specs=P(("row", "col"), None, None), check_vma=False
    )
```

```python
import jax
import jax.numpy as jnp
from jax import lax
from jax.experimental import pallas as pl
from jax.experimental.pallas import tpu as pltpu
from jax.sharding import PartitionSpec as P

MESH = pl.DeviceIdType.MESH
F32, BF16, I16, I32 = jnp.float32, jnp.bfloat16, jnp.int16, jnp.int32

K = 64
NRHS = 128
ELEM = 8
SLOTS = 512
HALF = SLOTS // 2
REACH = 3
SIDE = 4
COLS = SIDE * SIDE
GROUP = ELEM * COLS
WINDOW = ELEM * (REACH + 1)
QUART = ELEM // 2
UNROLL = 16
STEP = 32767.0
EXTRA = 16

LANES = 128
TILES = SLOTS // LANES
T_COL, T_ROW, T_PREV_ROW, T_PREV_COL = 0, TILES, 2 * TILES, 3 * TILES
T_LAST_ROW, T_LAST_COL = 4 * TILES, 4 * TILES + 2
T_ROWS = 4 * TILES + 8


def nn(a, b):
    return lax.dot_general(a, b, (((1,), (0,)), ((), ())), preferred_element_type=F32)


def nt(a, b):
    return lax.dot_general(a, b, (((1,), (1,)), ((), ())), preferred_element_type=F32)


def entry(table, name, i, u, half):
    per = LANES // UNROLL
    return table[name + half * (TILES // 2) + lax.div(i, per), lax.rem(i, per) * UNROLL + u]


def add_terms(i, terms, table, prev, hist):
    for u, pair in enumerate(terms):
        for half, term in enumerate(pair):
            hist[half * HALF + i * UNROLL + u] = term + hist[entry(table, prev, i, u, half)]


def row_terms(i, table, near, mats, hist):
    zero = jnp.zeros((K, NRHS), BF16)
    terms = []
    for u in range(UNROLL):
        one, two = (near[entry(table, T_COL, i, u, half)] for half in range(2))
        pair = mats[pl.ds(pl.multiple_of((i * UNROLL + u) * K, K), K), :].astype(BF16)
        both = jnp.concatenate(
            [jnp.concatenate([one, zero], 1), jnp.concatenate([zero, two], 1)], 0
        )
        t = nn(pair, both)
        terms.append((t[:, :NRHS], t[:, NRHS:]))
    add_terms(i, terms, table, T_PREV_ROW, hist)


def col_terms(i, table, group, mats, hist):
    terms = []
    for u in range(UNROLL):
        one, two = (group[entry(table, T_ROW, i, u, half)] for half in range(2))
        pair = mats[pl.ds(pl.multiple_of((i * UNROLL + u) * K, K), K), :].T.astype(BF16)
        terms.append((nn(pair[:K], one), nn(pair[K:], two)))
    add_terms(i, terms, table, T_PREV_COL, hist)


def total(table, name, e, hist):
    return hist[table[name, e]] + hist[table[name + 1, e]]


def tables(count_ref, rows_ref, cols_ref, out):
    rows, cols, count = rows_ref[...], cols_ref[...], count_ref[0]
    my_row = lax.axis_index("row")
    slot = lax.broadcasted_iota(I32, (TILES, LANES), 0) * LANES + lax.broadcasted_iota(I32, (TILES, LANES), 1)
    active = slot < count
    mirror = active & (rows != cols)
    row_local = jnp.clip(rows - my_row * GROUP, 0, GROUP - 1)
    col_local = (lax.shift_right_logical(cols, 7) - my_row) * ELEM + (cols & (ELEM - 1))
    col_local = jnp.clip(col_local, 0, WINDOW - 1)
    out[pl.ds(T_COL, TILES)] = col_local
    out[pl.ds(T_ROW, TILES)] = row_local
    out[pl.ds(T_LAST_COL + 2, T_ROWS - T_LAST_COL - 2)] = jnp.zeros((T_ROWS - T_LAST_COL - 2, LANES), I32)
    down = lax.broadcasted_iota(I32, (LANES, LANES), 0)
    across = lax.broadcasted_iota(I32, (LANES, LANES), 1)
    names = across.astype(F32)
    for key, prev, last in (
        (jnp.where(active, row_local, -1), T_PREV_ROW, T_LAST_ROW),
        (jnp.where(mirror, col_local, -1), T_PREV_COL, T_LAST_COL),
    ):
        key = key.astype(F32)
        wide = [jnp.broadcast_to(key[t : t + 1], (LANES, LANES)) for t in range(TILES)]
        tall = [w.T for w in wide]
        number = [(down + t * LANES).astype(F32) for t in range(TILES)]
        none = jnp.full((LANES, LANES), -1.0, F32)
        for half in range(2):
            low, high = 2 * half, 2 * half + 1
            found = []
            found.append(jnp.where((tall[low] == wide[low]) & (down < across), number[low], none))
            found.append(
                jnp.maximum(
                    jnp.where(tall[low] == wide[high], number[low], none),
                    jnp.where((tall[high] == wide[high]) & (down < across), number[high], none),
                )
            )
            ends = jnp.maximum(
                jnp.where(tall[low] == names, number[low], none),
                jnp.where(tall[high] == names, number[high], none),
            )
            for place, f in ((prev + low, found[0]), (prev + high, found[1]), (last + half, ends)):
                best = jnp.max(f, axis=0, keepdims=True)
                out[pl.ds(place, 1)] = jnp.where(best < 0, float(SLOTS), best).astype(I32)


def coded(values, out):
    n = len(values)
    peaks = [jnp.max(jnp.abs(v), axis=0, keepdims=True) for v in values]
    peaks.append(jnp.ones((EXTRA - n, NRHS), F32))
    power = jnp.ceil(jnp.log2(jnp.maximum(jnp.concatenate(peaks, axis=0), 1e-30)))
    out[pl.ds(n * K, EXTRA)] = power.astype(I32).astype(I16)
    scale = jnp.exp2(-power) * STEP
    for u, v in enumerate(values):
        out[pl.ds(u * K, K)] = jnp.round(v * scale[u : u + 1]).astype(I32).astype(I16)


def decoded(codes, n):
    step = jnp.exp2(codes[pl.ds(n * K, EXTRA)].astype(I32).astype(F32)) * (1.0 / STEP)
    return [codes[pl.ds(u * K, K)].astype(I32).astype(F32) * step[u : u + 1] for u in range(n)]


def kernel(
    table, coeffs, blocks, out, out_cols,
    flat, mats, hist, group, near, own,
    send1, got1, send2, got2, sendc, gotc, swap_out, swap_in, beside_out, beside_in,
    load_sem, ag_send, ag_recv, win_send, win_recv, s1_send, s1_recv, s2_send, s2_recv, c_send, c_recv,
):
    row, col = lax.axis_index("row"), lax.axis_index("col")
    n_row = lax.axis_size("row")
    core = lax.rem(row, 2)
    at = (lax.rem(col, SIDE), lax.div(col, SIDE))

    def place(k, a, b):
        return a * (1 + (SIDE - 1) * k) + b * (SIDE - (SIDE - 1) * k)

    def shift(v, by):
        return lax.rem(v + by + SIDE, SIDE)

    def send(src, dst, s, r, device):
        return pltpu.make_async_remote_copy(
            src_ref=src, dst_ref=dst, send_sem=s, recv_sem=r, device_id=device, device_id_type=MESH
        )

    barrier = pltpu.get_barrier_semaphore()
    for k in range(2):
        for by in range(1, SIDE):
            peer = place(k, shift(at[k], by), at[1 - k])
            pl.semaphore_signal(barrier, inc=1, device_id={"col": peer}, device_id_type=MESH)
    signals = 2 * (SIDE - 1)
    for o in range(1, REACH + 1):
        for r in (row - o, row + o):
            inside = (r >= 0) & (r < n_row)

            @pl.when(inside)
            def _(r=r):
                pl.semaphore_signal(barrier, inc=1, device_id={"row": r}, device_id_type=MESH)

            signals = signals + jnp.where(inside, 1, 0)

    chunk = K * K // 4
    loads = [
        pltpu.make_async_copy(
            blocks.at[pl.ds(i * chunk, chunk)], flat.at[pl.ds(i * chunk, chunk)], load_sem.at[i]
        )
        for i in range(4)
    ]
    for c in loads:
        c.start()
    loads += [
        pltpu.make_async_copy(coeffs, group.at[pl.ds(col * ELEM, ELEM)], load_sem.at[4]),
        pltpu.make_async_copy(coeffs, near.at[pl.ds(0, ELEM)], load_sem.at[5]),
    ]
    for c in loads[4:]:
        c.start()
    for o in range(1, REACH + 1):

        @pl.when(row + o >= n_row)
        def _(o=o):
            near[pl.ds(o * ELEM, ELEM)] = jnp.zeros((ELEM, K, NRHS), BF16)

    pl.semaphore_wait(barrier, signals)

    def window(o, src, s, peer):
        return send(src, near.at[pl.ds(o * ELEM, ELEM)], win_send.at[s], win_recv.at[o - 1], {"row": peer})

    second_row = near.at[pl.ds(2 * ELEM, ELEM)]
    passed = row + 2 < n_row
    windows = (
        (row >= 2, lambda: window(2, coeffs, 0, row - 2)),
        (core == 1, lambda: window(1, coeffs, 1, row - 1)),
        ((core == 0) & passed & (row >= 2), lambda: window(3, second_row, 1, row - 1)),
        ((core == 0) & passed, lambda: window(1, second_row, 2, row + 1)),
        ((core == 1) & passed, lambda: window(3, second_row, 2, row - 1)),
    )

    def window_arrived(o):
        @pl.when(row + o < n_row)
        def _():
            window(o, coeffs, 0, row).wait_recv()

    for when, make in windows[:2]:

        @pl.when(when)
        def _(make=make):
            make().start()

    def piece(k, da, db, part=None):
        dev = place(k, shift(at[k], da), shift(at[1 - k], db))
        if part is None:
            return group.at[pl.ds(dev * ELEM + k * QUART, QUART)]
        return group.at[pl.ds(dev * ELEM + k * QUART + part * (QUART // 2), QUART // 2)]

    started = []
    order = {0: 0, -1: 1, 1: 2, 2: 3}

    def gather(k, axis, da, db, part, to, index):
        a, b = (shift(at[k], to), at[1 - k]) if axis == 0 else (at[k], shift(at[1 - k], to))
        ref = piece(k, da, db, part)
        src = coeffs.at[pl.ds(k * QUART, QUART)] if da == 0 and db == 0 else ref
        c = send(src, ref, ag_send.at[k, index], ag_recv.at[k, index], {"col": place(k, a, b)})
        c.start()
        started.append(c)

    def arrived(k, da, db, part, index):
        ref = piece(k, da, db, part)
        send(ref, ref, ag_send.at[k, index], ag_recv.at[k, index], {"col": col}).wait_recv()

    def along(k, da):
        gather(k, 1, da, 0, None, 1, 3 + 4 * order[da])
        gather(k, 1, da, 0, None, -1, 4 + 4 * order[da])

    def across(k, da):
        arrived(k, da, -1, None, 3 + 4 * order[da])
        gather(k, 1, da, -1, 0, 1, 5 + 4 * order[da])
        arrived(k, da, 1, None, 4 + 4 * order[da])
        gather(k, 1, da, 1, 1, -1, 6 + 4 * order[da])

    def last(k, da):
        arrived(k, da, 2, 0, 5 + 4 * order[da])
        arrived(k, da, 2, 1, 6 + 4 * order[da])

    for k in range(2):
        gather(k, 0, 0, 0, None, 1, 0)
        gather(k, 0, 0, 0, None, -1, 1)
    for k in range(2):
        gather(k, 0, 0, 0, None, 2, 2)
    for k in range(2):
        along(k, 0)

    r = lax.broadcasted_iota(I32, (HALF, HALF), 0)
    c = lax.broadcasted_iota(I32, (HALF, HALF), 1)
    eye = jnp.where(r == c, 1.0, 0.0).astype(BF16)

    def turn(i, _):
        for u in range(8):
            j = i * 8 + u
            a = flat[pl.ds(pl.multiple_of(j * K, K), K), :]
            a = jnp.concatenate([a[:, :HALF], a[:, HALF:]], axis=0)
            mats[pl.ds(j, HALF, stride=K), :] = nt(eye, a)
        return 0

    for c in loads:
        c.wait()
    lax.fori_loop(0, 8, turn, 0)
    for k in range(2):
        arrived(k, -1, 0, None, 0)
        along(k, -1)
        arrived(k, 1, 0, None, 1)
        along(k, 1)
    window_arrived(2)
    for when, make in windows[2:]:

        @pl.when(when)
        def _(make=make):
            make().start()

    for k in range(2):
        arrived(k, 2, 0, None, 2)
        along(k, 2)
    for k in range(2):
        across(k, 0)
    window_arrived(1)
    window_arrived(3)

    hist[SLOTS] = jnp.zeros((K, NRHS), F32)

    def rows(i, _):
        row_terms(i, table, near, mats, hist)
        return 0

    steps = HALF // UNROLL
    lax.fori_loop(0, steps // 4, rows, 0)
    for k in range(2):
        across(k, -1)
        across(k, 1)
    lax.fori_loop(steps // 4, steps // 2, rows, 0)
    for k in range(2):
        across(k, 2)
    lax.fori_loop(steps // 2, steps, rows, 0)

    def first(k, d, bo, peer):
        return send(
            send1.at[k, d, bo], got1.at[k, d, bo], s1_send.at[k, d, bo], s1_recv.at[k, d, bo], {"col": peer}
        )

    def pick(k):
        return at[0] * (1 - k) + at[1] * k, at[1] * (1 - k) + at[0] * k

    for bo in (2, 1, 3, 0):

        def code(i, _, bo=bo):
            k, d = lax.rem(i, 2), lax.rem(lax.div(i, 2) + 1, SIDE - 1)
            mine_a, mine_b = pick(k)
            a, b = shift(mine_a, d + 1), shift(mine_b, bo)
            base = place(k, a, b) * ELEM + k * QUART
            coded([total(table, T_LAST_ROW, base + u, hist) for u in range(QUART)], send1.at[k, d, bo])
            first(k, d, bo, place(k, a, mine_b)).start()
            return 0

        lax.fori_loop(0, 2 * (SIDE - 1), code, 0)

    def keep(i, _):
        k, bo = lax.div(i, SIDE), lax.rem(i, SIDE)
        mine_a, mine_b = pick(k)
        base = place(k, mine_a, shift(mine_b, bo)) * ELEM + k * QUART
        for u in range(QUART):
            own[k, bo, u] = total(table, T_LAST_ROW, base + u, hist)
        return 0

    lax.fori_loop(0, 2 * SIDE, keep, 0)

    for k in range(2):
        for da in (0, -1, 1, 2):
            last(k, da)

    def cols(i, _):
        col_terms(i, table, group, mats, hist)
        return 0

    lax.fori_loop(0, steps, cols, 0)

    def swap(peer):
        return send(swap_out, swap_in, c_send.at[0], c_recv.at[0], {"row": peer})

    def beside(peer):
        return send(beside_out, beside_in, c_send.at[1], c_recv.at[1], {"row": peer})

    def column(i, peer):
        return send(sendc.at[i], gotc.at[i], c_send.at[2 + i], c_recv.at[2 + i], {"row": peer})

    other = row + 1 - 2 * core
    for u in range(ELEM):
        swap_out[u] = total(table, T_LAST_COL, (3 - 2 * core) * ELEM + u, hist)

    @pl.when(passed)
    def _():
        swap(other).start()

    @pl.when((core == 1) & (row + 3 < n_row))
    def _():
        coded([total(table, T_LAST_COL, 3 * ELEM + u, hist) for u in range(ELEM)], sendc.at[1])
        column(1, row + 3).start()

    @pl.when(core == 0)
    def _():
        for u in range(ELEM):
            beside_out[u] = total(table, T_LAST_COL, ELEM + u, hist)
        beside(row + 1).start()

    for u in range(ELEM):
        out_cols[u] = total(table, T_LAST_COL, u, hist)

    @pl.when(passed)
    def _():
        swap(other).wait_recv()
        coded([total(table, T_LAST_COL, 2 * ELEM + u, hist) + swap_in[u] for u in range(ELEM)], sendc.at[0])
        column(0, row + 2).start()

    def second(k, d, peer):
        return send(send2.at[k, d], got2.at[k, d], s2_send.at[k, d], s2_recv.at[k, d], {"col": peer})

    def gathered(k, bo):
        for d in range(SIDE - 1):
            first(k, d, bo, col).wait_recv()
        parts = [decoded(got1.at[k, d, bo], QUART) for d in range(SIDE - 1)]
        return [own[k, bo, u] + parts[0][u] + parts[1][u] + parts[2][u] for u in range(QUART)]

    for bo in (2, 1, 3):
        for k in range(2):
            coded(gathered(k, bo), send2.at[k, bo - 1])
            second(k, bo - 1, place(k, at[k], shift(at[1 - k], bo))).start()
    for k in range(2):
        for u, v in enumerate(gathered(k, 0)):
            out[k * QUART + u] = v

    @pl.when(core == 1)
    def _():
        beside(row).wait_recv()
        for u in range(ELEM):
            out_cols[u] += beside_in[u]

    for i, when in ((1, (core == 0) & (row >= 3)), (0, row >= 2)):

        @pl.when(when)
        def _(i=i):
            column(i, row).wait_recv()
            for u, v in enumerate(decoded(gotc.at[i], ELEM)):
                out_cols[u] += v

    for k in range(2):
        for d in range(SIDE - 1):
            second(k, d, col).wait_recv()
        parts = [decoded(got2.at[k, d], QUART) for d in range(SIDE - 1)]
        for u in range(QUART):
            out[k * QUART + u] += parts[0][u] + parts[1][u] + parts[2][u]

    for c in started:
        c.wait_send()
    for k in range(2):
        for d in range(SIDE - 1):
            for bo in range(SIDE):
                first(k, d, bo, col).wait_send()
            second(k, d, col).wait_send()
    for when, make in windows:

        @pl.when(when)
        def _(make=make):
            make().wait_send()

    @pl.when(passed)
    def _():
        for c in (swap(other), column(0, row)):
            c.wait_send()

    @pl.when((core == 1) & (row + 3 < n_row))
    def _():
        column(1, row).wait_send()

    @pl.when(core == 0)
    def _():
        beside(row).wait_send()


def body(coeffs, blocks, blk_rows, blk_cols, blk_count):
    flat = jnp.transpose(blocks, (1, 2, 0)).reshape(K * K, SLOTS)
    side = SIDE - 1
    vmem, dma = pltpu.VMEM, pltpu.SemaphoreType.DMA
    table = pl.pallas_call(
        tables,
        out_shape=jax.ShapeDtypeStruct((T_ROWS, LANES), I32),
        in_specs=[
            pl.BlockSpec(memory_space=pltpu.SMEM),
            pl.BlockSpec(memory_space=pltpu.VMEM),
            pl.BlockSpec(memory_space=pltpu.VMEM),
        ],
        out_specs=pl.BlockSpec(memory_space=pltpu.VMEM),
        name="tables",
    )(blk_count, blk_rows.reshape(TILES, LANES), blk_cols.reshape(TILES, LANES))
    sums, columns = pl.pallas_call(
        kernel,
        out_shape=(jax.ShapeDtypeStruct((ELEM, K, NRHS), F32),) * 2,
        in_specs=[
            pl.BlockSpec(memory_space=pltpu.SMEM),
            pl.BlockSpec(memory_space=pltpu.HBM),
            pl.BlockSpec(memory_space=pltpu.HBM),
        ],
        out_specs=(pl.BlockSpec(memory_space=pltpu.VMEM),) * 2,
        scratch_shapes=[
            vmem((K * K, SLOTS), BF16),
            vmem((HALF * K, 2 * K), F32),
            vmem((SLOTS + 1, K, NRHS), F32),
            vmem((GROUP, K, NRHS), BF16),
            vmem((WINDOW, K, NRHS), BF16),
            vmem((2, SIDE, QUART, K, NRHS), F32),
            *[vmem((2, side, SIDE, QUART * K + EXTRA, NRHS), I16)] * 2,
            *[vmem((2, side, QUART * K + EXTRA, NRHS), I16)] * 2,
            *[vmem((2, ELEM * K + EXTRA, NRHS), I16)] * 2,
            *[vmem((ELEM, K, NRHS), F32)] * 4,
            dma((6,)),
            dma((2, 19)),
            dma((2, 19)),
            dma((REACH,)),
            dma((REACH,)),
            dma((2, side, SIDE)),
            dma((2, side, SIDE)),
            dma((2, side)),
            dma((2, side)),
            dma((4,)),
            dma((4,)),
        ],
        compiler_params=pltpu.CompilerParams(
            collective_id=0, has_side_effects=True, vmem_limit_bytes=54 * 2**20
        ),
        name="near_field",
    )(table, coeffs, flat)
    return sums + columns


def solution(mesh):
    placed = (
        P(("row", "col"), None, None),
        P(("row", "col"), None, None),
        P(("row", "col")),
        P(("row", "col")),
        P(("row", "col")),
    )
    return jax.shard_map(
        body, mesh=mesh, in_specs=placed, out_specs=P(("row", "col"), None, None), check_vma=False
    )
```
